32 devices in a mesh: groups: 2 (over y), blk: 8 (over z, x), inner: 2 (over core).
Axes of the slice: x: 2, y: 2, z: 4, core: 2. Of those that a mesh axis runs over, the one named last changes fastest.
Arguments:
- inputs: float32 [32, 32768], P(None, ('groups', 'blk')), parts along dimension 1, may hold values from -6 to 6
- solved: float32 [16, 32768], P('inner', ('groups', 'blk')), parts along dimension 1, may hold values from -3.5 to 3.5
- probes: float32 [16, 32768], P('inner', ('groups', 'blk')), parts along dimension 1, may hold values from -6 to 6
- task_factor: float32 [16, 8], P('groups'), parts along dimension 0, may hold values from -2 to 2
- inv_len: float32 [64], P('groups'), parts along dimension 0, may hold values from 0.06 to 0.3
Outputs:
- window_grad: float32 [32, 32768], P(None, ('groups', 'blk', 'inner')), parts along dimension 1
The draws below stay inside these ranges and needn't reach their ends.
There are 2 independent parts, one for each index of `groups`. The reference program is written for one: setup_inputs(seed, part) draws one part's arguments, and reference() takes and returns one part's arrays. A program takes and returns all parts, laid end to end along the dimension named above; each array names one. Nothing has to cross between parts.
All inputs are finite; a program needn't handle non-finite values.
Results may differ from the reference program's by a relative error of at most 0.0003.
Values sent between devices are 32-bit elements; how exact they have to be, the bound alone decides.
A program may use at most 128 MiB of HBM per device.

```python
import math
import jax
import jax.numpy as jnp
from jax import lax

D = 32
TASKS = 8
PROBES = 2
REACH = 2
ROWS = 2048
NROWS = 16384
N_BLK = 8


def block_scale(own_key, extent, pieces, low, top_value):
    factor_of, own = 1.0, jax.random.fold_in(own_key, 6)
    for position, shards_of in pieces:
        draws = jnp.exp(jax.random.uniform(jax.random.fold_in(own, position), (shards_of,), jnp.float32, low / len(pieces), top_value / len(pieces)))
        factor_of = factor_of * jnp.repeat(draws, extent[position] // shards_of).reshape([-1 if axis == position else 1 for axis in range(len(extent))])
    return factor_of


def bell_draw(rng, extent, scale, most, pieces=(), kind=jnp.bfloat16):
    entries = jax.random.normal(rng, extent, jnp.float32) * scale
    if len(pieces) > 0:
        entries = block_scale(rng, extent, pieces, -0.22, 0.18) * entries
    return jnp.clip(entries, min=-most, max=most).astype(kind)


def setup_inputs(seed: int = 0, part: int = 0) -> dict:
    key_of = jax.random.split(jax.random.key(seed), 6)
    part_keys = jax.random.split(jax.random.fold_in(key_of[5], part), 6)
    return {
        "inputs": bell_draw(part_keys[0], (D, NROWS), 1.0, 6.0, ((1, 8),), jnp.float32),
        "solved": bell_draw(part_keys[1], (PROBES * TASKS, NROWS), (10.0 / ROWS ** 0.5), 3.5, ((0, 2), (1, 8)), jnp.float32),
        "probes": bell_draw(part_keys[2], (PROBES * TASKS, NROWS), 1.0, 6.0, ((0, 2), (1, 8)), jnp.float32),
        "task_factor": bell_draw(part_keys[3], (TASKS, TASKS), TASKS ** -0.5, 2.0, (), jnp.float32),
        "inv_len": jnp.clip(jnp.exp(jax.random.uniform(part_keys[4], (D,), jnp.float32, math.log(0.06), math.log(0.3))), 0.06, 0.3),
    }


precise = lax.Precision.HIGHEST


def fold_tasks(probes, task_factor):
    tasks = task_factor.shape[0]
    cov = jnp.dot(task_factor, task_factor.T, precision=precise, preferred_element_type=jnp.float32)
    shaped = probes.reshape(probes.shape[0] // tasks, tasks, probes.shape[1])
    folded = jnp.einsum("st,ptr->psr", cov, shaped, precision=precise)
    return folded.reshape(probes.shape[0], probes.shape[1])


def contract_first(left, right):
    return lax.dot_general(left, right, (((0,), (0,)), ((), ())), precision=precise, preferred_element_type=jnp.float32)


def pair_tile(rows, cols, weights, factor, want_cols):
    width = weights.shape[0]
    half = (cols.shape[0] - width) // 2
    x_cols = cols[:width]
    u_cols = cols[width:width + half]
    w_cols = cols[width + half:]
    norm_cols = jnp.sum(x_cols * x_cols * weights[:, None], axis=0)
    row_count = rows.shape[1]
    block_size = 1024 if row_count % 1024 == 0 else (512 if row_count % 512 == 0 else row_count)
    blocks = rows.reshape(rows.shape[0], row_count // block_size, block_size).transpose(1, 0, 2)
    coeff = -factor * weights[:, None]

    def block_pass(carried, block):
        x_rows = block[:width]
        u_rows = block[width:width + half]
        w_rows = block[width + half:]
        scaled = x_rows * weights[:, None]
        norm_rows = jnp.sum(x_rows * scaled, axis=0)
        cross = contract_first(scaled, x_cols)
        kernel = jnp.exp(-0.5 * (norm_rows[:, None] + norm_cols[None, :] - 2.0 * cross))
        pair_weight = contract_first(u_rows, w_cols) + contract_first(w_rows, u_cols)
        strength = pair_weight * kernel
        moved = lax.dot_general(x_cols, strength, (((1,), (1,)), ((), ())), precision=precise, preferred_element_type=jnp.float32)
        row_grad = coeff * (x_rows * jnp.sum(strength, axis=1)[None, :] - moved)
        if want_cols:
            pulled = jnp.dot(x_rows, strength, precision=precise, preferred_element_type=jnp.float32)
            carried = carried + coeff * (x_cols * jnp.sum(strength, axis=0)[None, :] - pulled)
        return carried, row_grad

    start_sum = jnp.zeros((width, cols.shape[1]), jnp.float32)
    col_grad, grads = lax.scan(block_pass, start_sum, blocks)
    row_total = grads.transpose(1, 0, 2).reshape(width, row_count)
    return row_total, col_grad


def reference(inputs, solved, probes, task_factor, inv_len):
    weights = inv_len * inv_len
    folded = fold_tasks(probes, task_factor)
    panel = jnp.concatenate([inputs, solved, folded], axis=0)

    def one_block(index):
        start = (index * ROWS).astype(jnp.int32)
        rows = lax.dynamic_slice_in_dim(panel, start, ROWS, 1)
        total = jnp.zeros((D, ROWS), jnp.float32)
        for offset in range(-REACH, REACH + 1):
            other = (((index + offset) % N_BLK) * ROWS).astype(jnp.int32)
            cols = lax.dynamic_slice_in_dim(panel, other, ROWS, 1)
            total = total + pair_tile(rows, cols, weights, 1.0 / PROBES, False)[0]
        return total

    grads = lax.map(one_block, jnp.arange(N_BLK, dtype=jnp.int32))
    return grads.transpose(1, 0, 2).reshape(D, N_BLK * ROWS)
```

```python
import functools
import math

import jax
import jax.numpy as jnp
from jax import lax
from jax.experimental import pallas as pl
from jax.experimental.pallas import tpu as pltpu
from jax.sharding import PartitionSpec as P

PROBES = 2
OFFSETS = (1, -1, 2, -2)
TI = 512
JC = 256
KDIM = 128
MESH = pl.DeviceIdType.MESH
ROOT = math.sqrt(math.log2(math.e))
F32 = jnp.float32
BF16 = jnp.bfloat16
precise = lax.Precision.HIGHEST


def split(value):
    high = value.astype(BF16).astype(F32)
    return high, (value - high).astype(BF16).astype(F32)


def split3(value):
    high = value.astype(BF16).astype(F32)
    rest = value - high
    mid = rest.astype(BF16).astype(F32)
    return high, mid, (rest - mid).astype(BF16).astype(F32)


def kernel(n_blk, x_ref, u_ref, v_ref, f_ref, len_ref, out_ref,
           xs, us, vs, own_u, own_v, a_exp, a_pair, b_exp, b_pair, b_y, acc, part, got,
           send_sem, recv_sem):
    grp = lax.axis_index("groups")
    blk = lax.axis_index("blk")
    me = lax.axis_index("inner")
    mate = 1 - me
    width, rows = x_ref.shape
    half = rows // 2
    tasks = u_ref.shape[0]

    barrier = pltpu.get_barrier_semaphore()
    pl.semaphore_signal(barrier, inc=1, device_id=(grp, blk, mate), device_id_type=MESH)
    for off in OFFSETS:
        other = lax.rem(blk + off + n_blk, n_blk)
        for inner in (me, mate):
            pl.semaphore_signal(barrier, inc=1, device_id=(grp, other, inner), device_id_type=MESH)
    pl.semaphore_wait(barrier, 1 + 2 * len(OFFSETS))

    def remote(src, dst, slot, kind, target):
        return pltpu.make_async_remote_copy(
            src_ref=src, dst_ref=dst, send_sem=send_sem.at[slot, kind], recv_sem=recv_sem.at[slot, kind],
            device_id=target, device_id_type=MESH)

    mine = pl.ds(pl.multiple_of(me * half, half), half)
    theirs = pl.ds(pl.multiple_of(mate * half, half), half)

    def copies(slot):
        far = len(OFFSETS)
        if isinstance(slot, int) and slot == far:
            partner = (grp, blk, mate)
            return [remote(u_ref, own_u.at[me], far, 0, partner), remote(v_ref, own_v.at[me], far, 1, partner)]
        target = lax.rem(blk - OFFSETS[slot] + n_blk, n_blk) if isinstance(slot, int) else lax.rem(blk + 1, n_blk)
        same, cross = (grp, target, me), (grp, target, mate)
        return [
            remote(x_ref.at[:, mine], xs.at[slot], slot, 0, same),
            remote(u_ref.at[:, mine], us.at[slot, me], slot, 1, same),
            remote(v_ref.at[:, mine], vs.at[slot, me], slot, 2, same),
            remote(u_ref.at[:, theirs], us.at[slot, me], slot, 3, cross),
            remote(v_ref.at[:, theirs], vs.at[slot, me], slot, 4, cross),
        ]

    partner_copies = copies(len(OFFSETS))
    for copy in partner_copies:
        copy.start()
    for slot in range(len(OFFSETS)):
        for copy in copies(slot):
            copy.start()

    own_u[me] = u_ref[...]
    own_v[me] = v_ref[...]
    square = (width, width)
    diag = lax.broadcasted_iota(jnp.int32, square, 0) == lax.broadcasted_iota(jnp.int32, square, 1)
    inv = jnp.sum(jnp.where(diag, jnp.broadcast_to(len_ref[...], square), 0.0), axis=1, keepdims=True)
    scale = inv * ROOT

    def norm_rows(y, ones_first):
        cols = y.shape[1]
        norm = jnp.broadcast_to(-0.5 * jnp.sum(y * y, axis=0, keepdims=True), (8, cols))
        high, mid, low = split3(norm)
        row = lax.broadcasted_iota(jnp.int32, (8, cols), 0)
        base = 3 if ones_first else 0
        ones = jnp.where((row < 3) if ones_first else (row >= 3) & (row < 6), 1.0, 0.0)
        picked = jnp.where(row == base, high, jnp.where(row == base + 1, mid, jnp.where(row == base + 2, low, ones)))
        return picked

    def prepare(slot, x, u0, u1, v0, v1):
        cols = x.shape[1]
        y = x * scale
        yh, yl = split(y)
        tail = jnp.zeros((KDIM - 3 * width - 8, cols), F32)
        b_exp[slot] = jnp.concatenate([yh, yl, yh, norm_rows(y, True), tail], axis=0).astype(BF16)
        one = jnp.where(lax.broadcasted_iota(jnp.int32, (16, cols), 0) == 0, 1.0, 0.0)
        b_y[slot] = jnp.concatenate([yh, yl, one], axis=0).astype(BF16)
        u = jnp.concatenate([u0, u1], axis=0)
        v = jnp.concatenate([v0, v1], axis=0)
        uh, ul = split(u)
        vh, vl = split(v)
        b_pair[slot] = jnp.concatenate([vh, vl, vh, uh, ul, uh], axis=0).astype(BF16)

    chunk = 512

    @pl.loop(0, rows // chunk)
    def _(index):
        at = pl.ds(pl.multiple_of(index * chunk, chunk), chunk)
        y = x_ref[:, at] * scale
        yh, yl = split(y)
        tail = jnp.zeros((KDIM - 3 * width - 8, chunk), F32)
        full = jnp.concatenate([yh, yh, yl, norm_rows(y, False), tail], axis=0)
        a_exp[at, :] = full.T.astype(BF16)

    factor = f_ref[...]
    cov = lax.dot_general(factor, factor, (((1,), (1,)), ((), ())), precision=precise, preferred_element_type=F32)

    for copy in partner_copies:
        copy.wait()

    def fold(ref, at):
        return jnp.concatenate(
            [jnp.dot(cov, ref[p, :, at], precision=precise, preferred_element_type=F32) for p in range(2)], axis=0)

    @pl.loop(0, rows // chunk)
    def _(index):
        at = pl.ds(pl.multiple_of(index * chunk, chunk), chunk)
        gh, gl = split(fold(own_u, at))
        wh, wl = split(fold(own_v, at))
        full = jnp.concatenate([gh, gh, gl, wh, wh, wl, jnp.zeros((KDIM - 12 * tasks, chunk), F32)], axis=0)
        a_pair[at, :] = full.T[:, : 12 * tasks].astype(BF16)

    def tiles(slot, first, start):
        @pl.loop(0, half // TI)
        def _(index):
            at = pl.ds(pl.multiple_of(start + index * TI, TI), TI)
            le = a_exp[at, :]
            lp = a_pair[at, :]
            total = None
            for c in range(half // JC):
                cols = pl.ds(c * JC, JC)
                expo = jnp.dot(le, b_exp[slot, :, cols], preferred_element_type=F32)
                pair = jnp.dot(lp, b_pair[slot, :, cols], preferred_element_type=F32)
                strength = jnp.exp2(expo) * pair
                high = strength.astype(BF16)
                low = (strength - high.astype(F32)).astype(BF16)
                right = b_y[slot, :, cols]
                dims = (((1,), (1,)), ((), ()))
                term = lax.dot_general(high, right, dims, preferred_element_type=F32)
                term = term + lax.dot_general(low, right, dims, preferred_element_type=F32)
                total = term if total is None else total + term
            if first:
                acc[at, :] = total
            else:
                acc[at, :] = acc[at, :] + total

    def gather(start):
        flat = acc[pl.ds(pl.multiple_of(start, half), half), :].T
        return flat[:width] + flat[width : 2 * width], flat[2 * width : 2 * width + 8]

    own = len(OFFSETS)
    prepare(own, x_ref[:, mine], own_u[0, :, mine], own_u[1, :, mine], own_v[0, :, mine], own_v[1, :, mine])
    tiles(own, True, mate * half)
    tiles(own, True, me * half)
    swap = remote(part, got, own, 2, (grp, blk, mate))
    for slot in range(len(OFFSETS)):
        for copy in copies(slot):
            copy.wait()
        prepare(slot, xs[slot], us[slot, 0], us[slot, 1], vs[slot, 0], vs[slot, 1])
        tiles(slot, False, mate * half)
        if slot == len(OFFSETS) - 1:
            moved, total = gather(mate * half)
            part[:width] = moved
            part[width:] = total
            swap.start()
        tiles(slot, False, me * half)
    moved, total = gather(me * half)
    swap.wait()
    moved = moved + got[:width]
    total = (total + got[width:])[:1]
    out_ref[...] = (inv * (-1.0 / (PROBES * ROOT))) * (x_ref[:, mine] * scale * total - moved)


def local(n_blk, inputs, solved, probes, task_factor, inv_len):
    width, rows = inputs.shape
    tasks = solved.shape[0]
    half = rows // 2
    near = len(OFFSETS)
    vmem = pl.BlockSpec(memory_space=pltpu.VMEM)
    pairs = 2 * rows * half * (2 * near + 2)
    return pl.pallas_call(
        functools.partial(kernel, n_blk),
        out_shape=jax.ShapeDtypeStruct((width, half), F32),
        in_specs=[vmem] * 5,
        out_specs=vmem,
        scratch_shapes=[
            pltpu.VMEM((near, width, half), F32),
            pltpu.VMEM((near, 2, tasks, half), F32),
            pltpu.VMEM((near, 2, tasks, half), F32),
            pltpu.VMEM((2, tasks, rows), F32),
            pltpu.VMEM((2, tasks, rows), F32),
            pltpu.VMEM((rows, KDIM), BF16),
            pltpu.VMEM((rows, 12 * tasks), BF16),
            pltpu.VMEM((near + 1, KDIM, half), BF16),
            pltpu.VMEM((near + 1, 12 * tasks, half), BF16),
            pltpu.VMEM((near + 1, 2 * width + 16, half), BF16),
            pltpu.VMEM((rows, 2 * width + 16), F32),
            pltpu.VMEM((width + 8, half), F32),
            pltpu.VMEM((width + 8, half), F32),
            pltpu.SemaphoreType.DMA((near + 1, 5)),
            pltpu.SemaphoreType.DMA((near + 1, 5)),
        ],
        compiler_params=pltpu.CompilerParams(
            collective_id=0, has_side_effects=True, vmem_limit_bytes=48 * 2**20),
        cost_estimate=pl.CostEstimate(flops=pairs * 128, bytes_accessed=2**20, transcendentals=pairs),
        name="window_grad",
    )(inputs, solved, probes, task_factor, inv_len.reshape(1, width))


def solution(mesh):
    placed = (
        P(None, ("groups", "blk")),
        P("inner", ("groups", "blk")),
        P("inner", ("groups", "blk")),
        P("groups", None),
        P("groups"),
    )
    return jax.shard_map(
        functools.partial(local, mesh.shape["blk"]),
        mesh=mesh,
        in_specs=placed,
        out_specs=P(None, ("groups", "blk", "inner")),
        check_vma=False,
    )
```

```python
import functools
import math

import jax
import jax.numpy as jnp
from jax import lax
from jax.experimental import pallas as pl
from jax.experimental.pallas import tpu as pltpu
from jax.sharding import PartitionSpec as P

PROBES = 2
NEAR = 4
TI = 1024
JC = 256
KDIM = 128
MESH = pl.DeviceIdType.MESH
ROOT = math.sqrt(math.log2(math.e))
F32 = jnp.float32
BF16 = jnp.bfloat16
precise = lax.Precision.HIGHEST


def split(value):
    high = value.astype(BF16).astype(F32)
    return high, (value - high).astype(BF16).astype(F32)


def split3(value):
    high = value.astype(BF16).astype(F32)
    rest = value - high
    mid = rest.astype(BF16).astype(F32)
    return high, mid, (rest - mid).astype(BF16).astype(F32)


def kernel(n_blk, x_hbm, u_hbm, v_hbm, f_hbm, len_hbm, out_ref,
           x_ref, f_ref, len_ref, xs, us, vs, own_u, own_v, a_exp, a_pair, b_exp, b_pair, b_y, acc, part, got,
           send_sem, recv_sem, local_sem):
    grp = lax.axis_index("groups")
    blk = lax.axis_index("blk")
    me = lax.axis_index("inner")
    mate = 1 - me
    width, rows = x_hbm.shape
    half = rows // 2
    tasks = u_hbm.shape[0]

    loads = [
        pltpu.make_async_copy(src, dst, local_sem.at[i])
        for i, (src, dst) in enumerate((
            (len_hbm, len_ref), (x_hbm, x_ref), (f_hbm, f_ref), (u_hbm, own_u.at[me]), (v_hbm, own_v.at[me])))
    ]
    for load in loads:
        load.start()

    side = 1 - 2 * lax.rem(blk, 2)
    beside = blk + side
    after = lax.rem(blk + 2, n_blk)
    before = lax.rem(blk + n_blk - 2, n_blk)
    far_up = lax.rem(blk + 2 * side + n_blk, n_blk)
    far_down = lax.rem(blk - 2 * side + n_blk, n_blk)

    barrier = pltpu.get_barrier_semaphore()
    pl.semaphore_signal(barrier, inc=1, device_id=(grp, blk, mate), device_id_type=MESH)
    for other in (beside, after, before):
        for inner in (me, mate):
            pl.semaphore_signal(barrier, inc=1, device_id=(grp, other, inner), device_id_type=MESH)
    pl.semaphore_wait(barrier, 7)

    def remote(src, dst, slot, kind, target):
        return pltpu.make_async_remote_copy(
            src_ref=src, dst_ref=dst, send_sem=send_sem.at[slot, kind], recv_sem=recv_sem.at[slot, kind],
            device_id=target, device_id_type=MESH)

    mine = pl.ds(pl.multiple_of(me * half, half), half)
    theirs = pl.ds(pl.multiple_of(mate * half, half), half)

    def copies(slot):
        if slot == 3:
            same = (grp, beside, me)
            return [remote(xs.at[1], xs.at[3], 3, 0, same),
                    remote(us.at[1], us.at[3], 3, 1, same),
                    remote(vs.at[1], vs.at[3], 3, 2, same)]
        target = (beside, far_down, far_up)[slot]
        same, cross = (grp, target, me), (grp, target, mate)
        return [
            remote(x_hbm.at[:, mine], xs.at[slot], slot, 0, same),
            remote(u_hbm.at[:, mine], us.at[slot, me], slot, 1, same),
            remote(v_hbm.at[:, mine], vs.at[slot, me], slot, 2, same),
            remote(u_hbm.at[:, theirs], us.at[slot, me], slot, 3, cross),
            remote(v_hbm.at[:, theirs], vs.at[slot, me], slot, 4, cross),
        ]

    partner = (grp, blk, mate)
    partner_copies = [remote(u_hbm, own_u.at[me], NEAR, 0, partner), remote(v_hbm, own_v.at[me], NEAR, 1, partner)]
    for copy in partner_copies:
        copy.start()
    for slot in (1, 0, 2):
        for copy in copies(slot):
            copy.start()

    for load in loads:
        load.wait()
    square = (width, width)
    diag = lax.broadcasted_iota(jnp.int32, square, 0) == lax.broadcasted_iota(jnp.int32, square, 1)
    inv = jnp.sum(jnp.where(diag, jnp.broadcast_to(len_ref[...], square), 0.0), axis=1, keepdims=True)
    scale = inv * ROOT

    def norm_rows(y, ones_first):
        cols = y.shape[1]
        norm = jnp.broadcast_to(-0.5 * jnp.sum(y * y, axis=0, keepdims=True), (8, cols))
        high, mid, low = split3(norm)
        row = lax.broadcasted_iota(jnp.int32, (8, cols), 0)
        base = 3 if ones_first else 0
        ones = jnp.where((row < 3) if ones_first else (row >= 3) & (row < 6), 1.0, 0.0)
        picked = jnp.where(row == base, high, jnp.where(row == base + 1, mid, jnp.where(row == base + 2, low, ones)))
        return picked

    def prepare(slot, x, u0, u1, v0, v1):
        cols = x.shape[1]
        y = x * scale
        yh, yl = split(y)
        tail = jnp.zeros((KDIM - 3 * width - 8, cols), F32)
        b_exp[slot] = jnp.concatenate([yh, yl, yh, norm_rows(y, True), tail], axis=0).astype(BF16)
        one = jnp.where(lax.broadcasted_iota(jnp.int32, (16, cols), 0) == 0, 1.0, 0.0)
        b_y[slot] = jnp.concatenate([yh, yl, one], axis=0).astype(BF16)
        u = jnp.concatenate([u0, u1], axis=0)
        v = jnp.concatenate([v0, v1], axis=0)
        uh, ul = split(u)
        vh, vl = split(v)
        b_pair[slot] = jnp.concatenate([vh, vl, vh, uh, ul, uh], axis=0).astype(BF16)

    chunk = 512

    @pl.loop(0, rows // chunk)
    def _(index):
        at = pl.ds(pl.multiple_of(index * chunk, chunk), chunk)
        y = x_ref[:, at] * scale
        yh, yl = split(y)
        tail = jnp.zeros((KDIM - 3 * width - 8, chunk), F32)
        full = jnp.concatenate([yh, yh, yl, norm_rows(y, False), tail], axis=0)
        a_exp[at, :] = full.T.astype(BF16)

    factor = f_ref[...]
    cov = lax.dot_general(factor, factor, (((1,), (1,)), ((), ())), precision=precise, preferred_element_type=F32)

    for copy in partner_copies:
        copy.wait()

    def fold(ref, at):
        parts = []
        for p in range(2):
            value = ref[p, :, at]
            parts.append(sum(cov[:, t : t + 1] * value[t : t + 1] for t in range(tasks)))
        return jnp.concatenate(parts, axis=0)

    @pl.loop(0, rows // chunk)
    def _(index):
        at = pl.ds(pl.multiple_of(index * chunk, chunk), chunk)
        gh, gl = split(fold(own_u, at))
        wh, wl = split(fold(own_v, at))
        full = jnp.concatenate([gh, gh, gl, wh, wh, wl, jnp.zeros((KDIM - 12 * tasks, chunk), F32)], axis=0)
        a_pair[at, :] = full.T[:, : 12 * tasks].astype(BF16)

    def tiles(slot, first, start):
        @pl.loop(0, half // TI)
        def _(index):
            at = pl.ds(pl.multiple_of(start + index * TI, TI), TI)
            le = a_exp[at, :]
            lp = a_pair[at, :]
            total = None
            for c in range(half // JC):
                cols = pl.ds(c * JC, JC)
                expo = jnp.dot(le, b_exp[slot, :, cols], preferred_element_type=F32)
                pair = jnp.dot(lp, b_pair[slot, :, cols], preferred_element_type=F32)
                strength = jnp.exp2(expo) * pair
                high = strength.astype(BF16)
                low = (strength - high.astype(F32)).astype(BF16)
                right = b_y[slot, :, cols]
                dims = (((1,), (1,)), ((), ()))
                term = lax.dot_general(high, right, dims, preferred_element_type=F32)
                term = term + lax.dot_general(low, right, dims, preferred_element_type=F32)
                total = term if total is None else total + term
            if first:
                acc[at, :] = total
            else:
                acc[at, :] = acc[at, :] + total

    def gather(start):
        flat = acc[pl.ds(pl.multiple_of(start, half), half), :].T
        return flat[:width] + flat[width : 2 * width], flat[2 * width : 2 * width + 8]

    own = NEAR
    prepare(own, x_ref[:, mine], own_u[0, :, mine], own_u[1, :, mine], own_v[0, :, mine], own_v[1, :, mine])
    tiles(own, True, mate * half)
    tiles(own, True, me * half)
    swap = remote(part, got, own, 2, (grp, blk, mate))
    for slot in range(NEAR):
        for copy in copies(slot):
            copy.wait()
        if slot == 1:
            for copy in copies(3):
                copy.start()
        prepare(slot, xs[slot], us[slot, 0], us[slot, 1], vs[slot, 0], vs[slot, 1])
        tiles(slot, False, mate * half)
        if slot == NEAR - 1:
            moved, total = gather(mate * half)
            part[:width] = moved
            part[width:] = total
            swap.start()
        tiles(slot, False, me * half)
    moved, total = gather(me * half)
    swap.wait()
    moved = moved + got[:width]
    total = (total + got[width:])[:1]
    out_ref[...] = (inv * (-1.0 / (PROBES * ROOT))) * (x_ref[:, mine] * scale * total - moved)


def local(n_blk, inputs, solved, probes, task_factor, inv_len):
    width, rows = inputs.shape
    tasks = solved.shape[0]
    half = rows // 2
    near = NEAR
    vmem = pl.BlockSpec(memory_space=pltpu.VMEM)
    pairs = 2 * rows * half * (2 * near + 2)
    return pl.pallas_call(
        functools.partial(kernel, n_blk),
        out_shape=jax.ShapeDtypeStruct((width, half), F32),
        in_specs=[pl.BlockSpec(memory_space=pltpu.HBM)] * 5,
        out_specs=vmem,
        scratch_shapes=[
            pltpu.VMEM((width, rows), F32),
            pltpu.VMEM((tasks, tasks), F32),
            pltpu.VMEM((1, width), F32),
            pltpu.VMEM((near, width, half), F32),
            pltpu.VMEM((near, 2, tasks, half), F32),
            pltpu.VMEM((near, 2, tasks, half), F32),
            pltpu.VMEM((2, tasks, rows), F32),
            pltpu.VMEM((2, tasks, rows), F32),
            pltpu.VMEM((rows, KDIM), BF16),
            pltpu.VMEM((rows, 12 * tasks), BF16),
            pltpu.VMEM((near + 1, KDIM, half), BF16),
            pltpu.VMEM((near + 1, 12 * tasks, half), BF16),
            pltpu.VMEM((near + 1, 2 * width + 16, half), BF16),
            pltpu.VMEM((rows, 2 * width + 16), F32),
            pltpu.VMEM((width + 8, half), F32),
            pltpu.VMEM((width + 8, half), F32),
            pltpu.SemaphoreType.DMA((near + 1, 5)),
            pltpu.SemaphoreType.DMA((near + 1, 5)),
            pltpu.SemaphoreType.DMA((5,)),
        ],
        compiler_params=pltpu.CompilerParams(
            collective_id=0, has_side_effects=True, vmem_limit_bytes=48 * 2**20),
        cost_estimate=pl.CostEstimate(flops=pairs * 128, bytes_accessed=2**20, transcendentals=pairs),
        name="window_grad",
    )(inputs, solved, probes, task_factor, inv_len.reshape(1, width))


def solution(mesh):
    placed = (
        P(None, ("groups", "blk")),
        P("inner", ("groups", "blk")),
        P("inner", ("groups", "blk")),
        P("groups", None),
        P("groups"),
    )
    return jax.shard_map(
        functools.partial(local, mesh.shape["blk"]),
        mesh=mesh,
        in_specs=placed,
        out_specs=P(None, ("groups", "blk", "inner")),
        check_vma=False,
    )
```

```python
import functools
import math

import jax
import jax.numpy as jnp
from jax import lax
from jax.experimental import pallas as pl
from jax.experimental.pallas import tpu as pltpu
from jax.sharding import PartitionSpec as P

PROBES = 2
NEAR = 4
TI = 1024
JC = 512
KDIM = 128
MESH = pl.DeviceIdType.MESH
ROOT = math.sqrt(math.log2(math.e))
F32 = jnp.float32
BF16 = jnp.bfloat16
precise = lax.Precision.HIGHEST


def split(value):
    high = value.astype(BF16).astype(F32)
    return high, (value - high).astype(BF16).astype(F32)


def split3(value):
    high = value.astype(BF16).astype(F32)
    rest = value - high
    mid = rest.astype(BF16).astype(F32)
    return high, mid, (rest - mid).astype(BF16).astype(F32)


def kernel(n_blk, x_hbm, u_hbm, v_hbm, f_hbm, len_hbm, out_ref,
           x_ref, f_ref, len_ref, xs, us, vs, own_u, own_v, a_exp, a_pair, b_exp, b_pair, b_y, acc, part, got,
           send_sem, recv_sem, local_sem):
    grp = lax.axis_index("groups")
    blk = lax.axis_index("blk")
    me = lax.axis_index("inner")
    mate = 1 - me
    width, rows = x_hbm.shape
    half = rows // 2
    tasks = u_hbm.shape[0]

    loads = [
        pltpu.make_async_copy(src, dst, local_sem.at[i])
        for i, (src, dst) in enumerate((
            (len_hbm, len_ref), (x_hbm, x_ref), (f_hbm, f_ref), (u_hbm, own_u.at[me]), (v_hbm, own_v.at[me])))
    ]
    for load in loads:
        load.start()

    side = 1 - 2 * lax.rem(blk, 2)
    beside = blk + side
    after = lax.rem(blk + 2, n_blk)
    before = lax.rem(blk + n_blk - 2, n_blk)
    far_up = lax.rem(blk + 2 * side + n_blk, n_blk)
    far_down = lax.rem(blk - 2 * side + n_blk, n_blk)

    barrier = pltpu.get_barrier_semaphore()
    pl.semaphore_signal(barrier, inc=1, device_id=(grp, blk, mate), device_id_type=MESH)
    for other in (beside, after, before):
        for inner in (me, mate):
            pl.semaphore_signal(barrier, inc=1, device_id=(grp, other, inner), device_id_type=MESH)
    pl.semaphore_wait(barrier, 7)

    def remote(src, dst, slot, kind, target):
        return pltpu.make_async_remote_copy(
            src_ref=src, dst_ref=dst, send_sem=send_sem.at[slot, kind], recv_sem=recv_sem.at[slot, kind],
            device_id=target, device_id_type=MESH)

    mine = pl.ds(pl.multiple_of(me * half, half), half)
    theirs = pl.ds(pl.multiple_of(mate * half, half), half)

    def copies(slot):
        if slot == 3:
            same = (grp, beside, me)
            return [remote(xs.at[1], xs.at[3], 3, 0, same),
                    remote(us.at[1], us.at[3], 3, 1, same),
                    remote(vs.at[1], vs.at[3], 3, 2, same)]
        target = (beside, far_down, far_up)[slot]
        same, cross = (grp, target, me), (grp, target, mate)
        return [
            remote(x_hbm.at[:, mine], xs.at[slot], slot, 0, same),
            remote(u_hbm.at[:, mine], us.at[slot, me], slot, 1, same),
            remote(v_hbm.at[:, mine], vs.at[slot, me], slot, 2, same),
            remote(u_hbm.at[:, theirs], us.at[slot, me], slot, 3, cross),
            remote(v_hbm.at[:, theirs], vs.at[slot, me], slot, 4, cross),
        ]

    partner = (grp, blk, mate)
    partner_copies = [remote(u_hbm, own_u.at[me], NEAR, 0, partner), remote(v_hbm, own_v.at[me], NEAR, 1, partner)]
    for copy in partner_copies:
        copy.start()
    for slot in (1, 0, 2):
        for copy in copies(slot):
            copy.start()

    for load in loads:
        load.wait()
    square = (width, width)
    diag = lax.broadcasted_iota(jnp.int32, square, 0) == lax.broadcasted_iota(jnp.int32, square, 1)
    inv = jnp.sum(jnp.where(diag, jnp.broadcast_to(len_ref[...], square), 0.0), axis=1, keepdims=True)
    scale = inv * ROOT

    def norm_rows(y, ones_first):
        cols = y.shape[1]
        norm = jnp.broadcast_to(-0.5 * jnp.sum(y * y, axis=0, keepdims=True), (8, cols))
        high, mid, low = split3(norm)
        row = lax.broadcasted_iota(jnp.int32, (8, cols), 0)
        base = 3 if ones_first else 0
        ones = jnp.where((row < 3) if ones_first else (row >= 3) & (row < 6), 1.0, 0.0)
        picked = jnp.where(row == base, high, jnp.where(row == base + 1, mid, jnp.where(row == base + 2, low, ones)))
        return picked

    def prepare(slot, x, u0, u1, v0, v1):
        cols = x.shape[1]
        y = x * scale
        yh, yl = split(y)
        tail = jnp.zeros((KDIM - 3 * width - 8, cols), F32)
        b_exp[slot] = jnp.concatenate([yh, yl, yh, norm_rows(y, True), tail], axis=0).T.astype(BF16)
        one = jnp.where(lax.broadcasted_iota(jnp.int32, (16, cols), 0) == 0, 1.0, 0.0)
        b_y[slot] = jnp.concatenate([yh, yl, one], axis=0).astype(BF16)
        u = jnp.concatenate([u0, u1], axis=0)
        v = jnp.concatenate([v0, v1], axis=0)
        uh, ul = split(u)
        vh, vl = split(v)
        pair = jnp.concatenate([vh, vl, vh, uh, ul, uh, jnp.zeros((KDIM - 12 * tasks, cols), F32)], axis=0)
        b_pair[slot] = pair.T[:, : 12 * tasks].astype(BF16)

    chunk = 512

    @pl.loop(0, rows // chunk)
    def _(index):
        at = pl.ds(pl.multiple_of(index * chunk, chunk), chunk)
        y = x_ref[:, at] * scale
        yh, yl = split(y)
        tail = jnp.zeros((KDIM - 3 * width - 8, chunk), F32)
        full = jnp.concatenate([yh, yh, yl, norm_rows(y, False), tail], axis=0)
        a_exp[:, at] = full.astype(BF16)

    factor = f_ref[...]
    cov = lax.dot_general(factor, factor, (((1,), (1,)), ((), ())), precision=precise, preferred_element_type=F32)

    for copy in partner_copies:
        copy.wait()

    def fold(ref, at):
        parts = []
        for p in range(2):
            value = ref[p, :, at]
            parts.append(sum(cov[:, t : t + 1] * value[t : t + 1] for t in range(tasks)))
        return jnp.concatenate(parts, axis=0)

    @pl.loop(0, rows // chunk)
    def _(index):
        at = pl.ds(pl.multiple_of(index * chunk, chunk), chunk)
        gh, gl = split(fold(own_u, at))
        wh, wl = split(fold(own_v, at))
        full = jnp.concatenate([gh, gh, gl, wh, wh, wl, jnp.zeros((KDIM - 12 * tasks, chunk), F32)], axis=0)
        a_pair[:, at] = full[: 12 * tasks].astype(BF16)

    def tiles(slot, first, start):
        @pl.loop(0, half // TI)
        def _(index):
            left = b_y[slot]
            for c in range(TI // JC):
                at = pl.ds(pl.multiple_of(start + index * TI + c * JC, JC), JC)
                expo = jnp.dot(b_exp[slot], a_exp[:, at], preferred_element_type=F32)
                pair = jnp.dot(b_pair[slot], a_pair[:, at], preferred_element_type=F32)
                strength = jnp.exp2(expo) * pair
                high = strength.astype(BF16)
                low = (strength - high.astype(F32)).astype(BF16)
                total = jnp.dot(left, high, preferred_element_type=F32)
                total = total + jnp.dot(left, low, preferred_element_type=F32)
                if first:
                    acc[:, at] = total
                else:
                    acc[:, at] = acc[:, at] + total

    def gather(start):
        flat = acc[:, pl.ds(pl.multiple_of(start, half), half)]
        return flat[:width] + flat[width : 2 * width], flat[2 * width : 2 * width + 8]

    own = NEAR
    prepare(own, x_ref[:, mine], own_u[0, :, mine], own_u[1, :, mine], own_v[0, :, mine], own_v[1, :, mine])
    tiles(own, True, mate * half)
    tiles(own, True, me * half)
    swap = remote(part, got, own, 2, (grp, blk, mate))
    for slot in range(NEAR):
        for copy in copies(slot):
            copy.wait()
        if slot == 1:
            for copy in copies(3):
                copy.start()
        prepare(slot, xs[slot], us[slot, 0], us[slot, 1], vs[slot, 0], vs[slot, 1])
        tiles(slot, False, mate * half)
        if slot == NEAR - 1:
            moved, total = gather(mate * half)
            part[:width] = moved
            part[width:] = total
            swap.start()
        tiles(slot, False, me * half)
    moved, total = gather(me * half)
    swap.wait()
    moved = moved + got[:width]
    total = (total + got[width:])[:1]
    out_ref[...] = (inv * (-1.0 / (PROBES * ROOT))) * (x_ref[:, mine] * scale * total - moved)


def local(n_blk, inputs, solved, probes, task_factor, inv_len):
    width, rows = inputs.shape
    tasks = solved.shape[0]
    half = rows // 2
    near = NEAR
    vmem = pl.BlockSpec(memory_space=pltpu.VMEM)
    pairs = 2 * rows * half * (2 * near + 2)
    return pl.pallas_call(
        functools.partial(kernel, n_blk),
        out_shape=jax.ShapeDtypeStruct((width, half), F32),
        in_specs=[pl.BlockSpec(memory_space=pltpu.HBM)] * 5,
        out_specs=vmem,
        scratch_shapes=[
            pltpu.VMEM((width, rows), F32),
            pltpu.VMEM((tasks, tasks), F32),
            pltpu.VMEM((1, width), F32),
            pltpu.VMEM((near, width, half), F32),
            pltpu.VMEM((near, 2, tasks, half), F32),
            pltpu.VMEM((near, 2, tasks, half), F32),
            pltpu.VMEM((2, tasks, rows), F32),
            pltpu.VMEM((2, tasks, rows), F32),
            pltpu.VMEM((KDIM, rows), BF16),
            pltpu.VMEM((12 * tasks, rows), BF16),
            pltpu.VMEM((near + 1, half, KDIM), BF16),
            pltpu.VMEM((near + 1, half, 12 * tasks), BF16),
            pltpu.VMEM((near + 1, 2 * width + 16, half), BF16),
            pltpu.VMEM((2 * width + 16, rows), F32),
            pltpu.VMEM((width + 8, half), F32),
            pltpu.VMEM((width + 8, half), F32),
            pltpu.SemaphoreType.DMA((near + 1, 5)),
            pltpu.SemaphoreType.DMA((near + 1, 5)),
            pltpu.SemaphoreType.DMA((5,)),
        ],
        compiler_params=pltpu.CompilerParams(
            collective_id=0, has_side_effects=True, vmem_limit_bytes=48 * 2**20),
        cost_estimate=pl.CostEstimate(flops=pairs * 128, bytes_accessed=2**20, transcendentals=pairs),
        name="window_grad",
    )(inputs, solved, probes, task_factor, inv_len.reshape(1, width))


def solution(mesh):
    placed = (
        P(None, ("groups", "blk")),
        P("inner", ("groups", "blk")),
        P("inner", ("groups", "blk")),
        P("groups", None),
        P("groups"),
    )
    return jax.shard_map(
        functools.partial(local, mesh.shape["blk"]),
        mesh=mesh,
        in_specs=placed,
        out_specs=P(None, ("groups", "blk", "inner")),
        check_vma=False,
    )
```
